128 devices in a mesh: lat: 8 (over x, core), wid: 16 (over z, y).
Axes of the slice: x: 4, y: 4, z: 4, core: 2. Of those that a mesh axis runs over, the one named last changes fastest.
Arguments:
- residual: bfloat16 [512, 8192], P(None, 'wid'), may hold values from -6 to 6
- dec_bias: float32 [8192], P('wid'), may hold values from -3 to 3
- enc_weight: bfloat16 [8192, 32768], P('wid', 'lat'), may hold values from -0.0625 to 0.0625
- enc_bias: float32 [32768], P('lat'), may hold values from -3 to 3
- dec_weight: bfloat16 [32768, 8192], P('lat', 'wid'), may hold values from -0.046875 to 0.046875
- act_mask: int32 [512, 32768], P(None, 'lat'), may hold values 0 or 1
- boundaries: int32 [8], replicated, may hold values from 1 to 32768, as said below
Outputs:
- grad_enc: bfloat16 [8192, 32768], P('wid', 'lat')
- grad_dec: bfloat16 [32768, 8192], P('lat', 'wid')
- grad_benc: float32 [32768], P('lat')
The draws below stay inside these ranges and needn't reach their ends.
Inputs may be any that keep to these rules, and one draw needn't show every extreme that they name: Strictly increasing; boundaries[k] lies above k * 4096 and at most (k + 1) * 4096; the last equals 32768.
All inputs are finite; a program needn't handle non-finite values. No bound on the sum of `act_mask` on one device may be relied on, other than what follows from the above.
Results may differ from the reference program's by a relative error of at most 0.006.
Values may be sent and summed in bfloat16 or wider, within the bound.
No kernel may reach another device: no remote copies, remote signals or barrier semaphores. Data moves between devices by JAX's collectives and lax.ppermute only.
A program may use at most 128 MiB of HBM per device.

```python
import jax
import jax.numpy as jnp
from jax import lax

D = 8192
L = 32768
K = 8
R = 512


def draw_boundaries(key, part):
    key = jax.random.fold_in(key, 7)
    width = L // K
    offsets = jax.random.randint(key, (K,), 1, width + 1)
    order = jnp.arange(K, dtype=jnp.int32)
    bounds = order * width + offsets
    return jnp.where(order == K - 1, L, bounds).astype(jnp.int32)


def set_ends(array, stream_key, least, high):
    longest = array.shape.index(max(array.shape))
    spots = []
    for shift in (0, 1):
        where = [jax.random.randint(jax.random.fold_in(stream_key, axis), (), 0, length) for axis, length in enumerate(array.shape)]
        where[longest] = (where[longest] + shift) % array.shape[longest]
        spots.append(tuple(where))
    return array.at[spots[0]].set(least).at[spots[1]].set(high)


def level_of(rng, shape, split, least, largest):
    def one(dim, blocks):
        draws = jax.random.uniform(jax.random.fold_in(jax.random.fold_in(rng, 6), dim), (blocks,), jnp.float32, least / len(split), largest / len(split))
        return jnp.repeat(jnp.exp(draws), shape[dim] // blocks).reshape((-1,) + (1,) * (len(shape) - dim - 1))

    gain = one(*split[0])
    for cut in split[1:]:
        gain = gain * one(*cut)
    return gain


def bell_draw(rng, shape, deviation, most, split=(), held_as=jnp.bfloat16):
    values = deviation * jax.random.normal(rng, shape, jnp.float32)
    if split:
        values = values * level_of(rng, shape, split, -0.22, 0.18)
    return jnp.clip(values, -most, most).astype(held_as)


def setup_inputs(seed: int = 0) -> dict:
    splits = jax.random.split(jax.random.key(seed), 8)
    return {
        "residual": bell_draw(splits[0], (R, D), 1.0, 6.0, ((1, 16),)),
        "dec_bias": bell_draw(splits[1], (D,), 0.5, 3.0, ((0, 16),), jnp.float32),
        "enc_weight": bell_draw(splits[2], (D, L), D ** -0.5, 0.0625, ((0, 16), (1, 8))),
        "enc_bias": bell_draw(splits[3], (L,), 0.5, 3.0, ((0, 8),), jnp.float32),
        "dec_weight": bell_draw(splits[4], (L, D), (L // 2) ** -0.5, 0.046875, ((0, 8), (1, 16))),
        "act_mask": set_ends((jax.random.randint(splits[5], (R, L), 0, 2) < 1).astype(jnp.int32), jax.random.fold_in(splits[5], 1), 0, 1),
        "boundaries": draw_boundaries(jax.random.fold_in(splits[7], 71), 0),
    }


def reference(residual, dec_bias, enc_weight, enc_bias, dec_weight, act_mask, boundaries):
    rows = residual.shape[0]
    scale = 2.0 / rows
    resid_f = residual.astype(jnp.float32)
    centred = (resid_f - dec_bias).astype(jnp.bfloat16)
    preact = jnp.dot(centred, enc_weight, preferred_element_type=jnp.float32) + enc_bias
    latents = (act_mask.astype(jnp.float32) * preact).astype(jnp.bfloat16)
    tile = min(1024, L // K)
    tiles = L // tile

    def tile_total(carry, index):
        start = (index * tile).astype(jnp.int32)
        piece = lax.dynamic_slice_in_dim(latents, start, tile, 1)
        weights = lax.dynamic_slice_in_dim(dec_weight, start, tile, 0)
        total = carry + jnp.dot(piece, weights, preferred_element_type=jnp.float32)
        return total, carry

    final, before = lax.scan(tile_total, jnp.zeros((rows, D), jnp.float32), jnp.arange(tiles, dtype=jnp.int32))

    def error_of(bound):
        index = ((bound - 1) // tile).astype(jnp.int32)
        start = (index * tile).astype(jnp.int32)
        piece = lax.dynamic_slice_in_dim(latents, start, tile, 1)
        weights = lax.dynamic_slice_in_dim(dec_weight, start, tile, 0)
        keep = (start + jnp.arange(tile, dtype=jnp.int32) < bound).astype(jnp.bfloat16)
        partial_value = jnp.dot(piece * keep[None, :], weights, preferred_element_type=jnp.float32)
        earlier = lax.dynamic_index_in_dim(before, index, 0, keepdims=False)
        return dec_bias + earlier + partial_value - resid_f

    errors = lax.map(error_of, boundaries)
    levels = jnp.flip(jnp.cumsum(jnp.flip(errors, 0), 0), 0).astype(jnp.bfloat16)

    def tile_grads(carry, index):
        start = (index * tile).astype(jnp.int32)
        position = start + jnp.arange(tile, dtype=jnp.int32)
        segment = jnp.sum((boundaries[:, None] <= position[None, :]).astype(jnp.int32), axis=0)
        lower = jnp.sum((boundaries <= start).astype(jnp.int32)).astype(jnp.int32)
        upper = jnp.minimum(lower + 1, K - 1).astype(jnp.int32)
        level_low = lax.dynamic_index_in_dim(levels, lower, 0, keepdims=False)
        level_high = lax.dynamic_index_in_dim(levels, upper, 0, keepdims=False)
        piece = lax.dynamic_slice_in_dim(latents, start, tile, 1)
        weights = lax.dynamic_slice_in_dim(dec_weight, start, tile, 0)
        mask_tile = lax.dynamic_slice_in_dim(act_mask, start, tile, 1)
        chosen = segment == lower
        through_low = jnp.dot(level_low, weights.T, preferred_element_type=jnp.float32)
        through_high = jnp.dot(level_high, weights.T, preferred_element_type=jnp.float32)
        grad_latent = scale * jnp.where(chosen[None, :], through_low, through_high)
        grad_pre = (mask_tile.astype(jnp.float32) * grad_latent).astype(jnp.bfloat16)
        outer_low = jnp.dot(piece.T, level_low, preferred_element_type=jnp.float32)
        outer_high = jnp.dot(piece.T, level_high, preferred_element_type=jnp.float32)
        grad_dec_tile = (scale * jnp.where(chosen[:, None], outer_low, outer_high)).astype(jnp.bfloat16)
        grad_enc_tile = jnp.dot(centred.T, grad_pre, preferred_element_type=jnp.float32).astype(jnp.bfloat16)
        grad_bias_tile = jnp.sum(grad_pre.astype(jnp.float32), axis=0)
        return carry, (grad_enc_tile, grad_dec_tile, grad_bias_tile)

    carry_out, outputs = lax.scan(tile_grads, jnp.zeros((), jnp.float32), jnp.arange(tiles, dtype=jnp.int32))
    enc_tiles, dec_tiles, bias_tiles = outputs
    grad_enc = jnp.transpose(enc_tiles, (1, 0, 2)).reshape(D, L)
    grad_dec = dec_tiles.reshape(L, D)
    grad_benc = bias_tiles.reshape(L)
    return grad_enc, grad_dec, grad_benc
```

```python
import jax
import jax.numpy as jnp
from jax import lax
from jax.sharding import Mesh, PartitionSpec as P

F32 = jnp.float32
BF16 = jnp.bfloat16
ALL = ("x", "core", "z", "y")
SIZES = (4, 2, 4, 4)
CHUNKS = 2


def place(x, c, z, y):
    return ((x * 2 + c) * 4 + z) * 4 + y


def every():
    return [(x, c, z, y) for x in range(4) for c in range(2) for z in range(4) for y in range(4)]


def ring_perm(shift):
    pairs = []
    for x, c, z, y in every():
        to = place(x, c, z, (y + shift) % 4) if c == 0 else place(x, c, (z + shift) % 4, y)
        pairs.append((place(x, c, z, y), to))
    return pairs


def swap_perm(kind):
    other = ((1, 0, 3, 2), (3, 2, 1, 0))[kind]
    pairs = []
    for x, c, z, y in every():
        to = place(x, c, other[z], y) if c == 0 else place(x, c, z, other[y])
        pairs.append((place(x, c, z, y), to))
    return pairs


def rounded(value):
    return lax.reduce_precision(value, 8, 7)


def scatter_out(partial_value):
    q = partial_value.shape[0] // 4
    sent = [partial_value[k * q : (k + 1) * q].astype(BF16) for k in (1, 2, 3)]
    return partial_value[:q], sent


def scatter_move(own, sent):
    got = [lax.ppermute(s, ALL, ring_perm(k)) for k, s in zip((1, 2, 3), sent)]
    return own + got[0].astype(F32) + got[1].astype(F32) + got[2].astype(F32)


def inner_sum(value):
    for kind in (0, 1):
        mine = rounded(value)
        got = lax.ppermute(mine.astype(BF16), ALL, swap_perm(kind))
        value = mine + got.astype(F32)
    return value


def gather_out(own):
    return [own] + [lax.ppermute(own, ALL, ring_perm(-k)) for k in (1, 2, 3)]


def turn(value, blocks, axis=0):
    size = value.shape[axis]
    twice = jnp.concatenate([value, value], axis)
    return lax.dynamic_slice_in_dim(twice, blocks * (size // 4), size, axis)


def shards(residual, dec_bias, enc_weight, enc_bias, dec_weight, act_mask, boundaries):
    rows = residual.shape[0]
    block = enc_weight.shape[1]
    x, c, z, y = (lax.axis_index(a) for a in ALL)
    lat_index = x * 2 + c
    outer = jnp.where(c == 0, y, z)
    outer_there = jnp.where(c == 0, z, y)
    scale = 2.0 / rows
    n = rows // CHUNKS
    q = n // 4
    order = jnp.arange(boundaries.shape[0], dtype=jnp.int32)
    offset = jnp.sum(jnp.where(order == lat_index, boundaries, 0)) - lat_index * block
    column = jnp.arange(block, dtype=jnp.int32)
    low = column < offset
    keep = low.astype(BF16)
    above = (7 - lat_index).astype(F32)

    state = []
    for k in range(CHUNKS):
        resid = turn(residual[k * n : (k + 1) * n], outer).astype(F32)
        base = dec_bias - resid
        centred = (resid - dec_bias).astype(BF16)
        mask = lax.dynamic_slice_in_dim(act_mask, k * n + outer * q, q, 0) != 0
        state.append(dict(base=base, centred=centred, mask=mask))

    def encode(s):
        s["own"], s["sent"] = scatter_out(jnp.dot(s["centred"], enc_weight, preferred_element_type=F32))

    def move(s):
        s["sum"] = scatter_move(s["own"], s["sent"])

    def latent_sum(s):
        preact = inner_sum(s["sum"]) + enc_bias
        s["mine"] = jnp.where(s["mask"], preact, 0.0).astype(BF16)

    def latent_gather(s):
        s["latents"] = jnp.concatenate(gather_out(s["mine"]), 0)

    def decode(s):
        latents = s["latents"]
        total = jnp.dot(latents, dec_weight, preferred_element_type=F32)
        lower = jnp.dot(latents * keep[None, :], dec_weight, preferred_element_type=F32)
        upper = above * total + lower
        total_b, upper_b = total.astype(BF16), upper.astype(BF16)
        before, after = 0.0, 0.0
        for k in (1, 2, 3):
            out = jnp.where(x + k < 4, total_b, upper_b)
            got = lax.ppermute(out, "x", [(i, (i + k) % 4) for i in range(4)]).astype(F32)
            before = before + jnp.where(x >= k, got, 0.0)
            after = after + jnp.where(x < k, got, 0.0)
        give = jnp.stack([before + jnp.where(c == 0, total, 0.0), after + jnp.where(c == 1, upper, 0.0)])
        got = lax.ppermute(turn(give, jnp.mod(outer_there - outer, 4), 1), "core", [(0, 1), (1, 0)])
        before = s["base"] + before + got[0]
        after = after + got[1]
        s["level_low"] = ((above + 1.0) * before + upper + after).astype(BF16)
        s["level_high"] = (above * (before + total) + after).astype(BF16)

    def through(s):
        dims = (((1,), (1,)), ((), ()))
        one = lax.dot_general(s["level_low"], dec_weight, dims, preferred_element_type=F32)
        two = lax.dot_general(s["level_high"], dec_weight, dims, preferred_element_type=F32)
        s["own"], s["sent"] = scatter_out(jnp.where(low[None, :], one, two))

    def grad_sum(s):
        total = scale * inner_sum(s["sum"])
        s["mine"] = jnp.where(s["mask"], total, 0.0).astype(BF16)

    def grad_gather(s):
        s["grad_pre"] = jnp.concatenate(gather_out(s["mine"]), 0)

    for stage in (encode, move, latent_sum, latent_gather, decode, through, move, grad_sum, grad_gather):
        for s in state:
            stage(s)

    def whole(name):
        return jnp.concatenate([s[name] for s in state], 0)

    dims = (((0,), (0,)), ((), ()))
    latents = whole("latents")
    one = lax.dot_general(latents, whole("level_low"), dims, preferred_element_type=F32)
    two = lax.dot_general(latents, whole("level_high"), dims, preferred_element_type=F32)
    grad_dec = (scale * jnp.where(low[:, None], one, two)).astype(BF16)
    grad_pre = whole("grad_pre")
    grad_enc = lax.dot_general(whole("centred"), grad_pre, dims, preferred_element_type=F32).astype(BF16)
    sums = jnp.sum(grad_pre.astype(F32).reshape(CHUNKS, 4, q, block), axis=2)
    sums = turn(sums, jnp.mod(-outer, 4), 1).reshape(CHUNKS * 4, block)
    grad_benc = sums[0]
    for k in range(1, CHUNKS * 4):
        grad_benc = grad_benc + sums[k]
    return (grad_enc, grad_dec, grad_benc)


def solution(mesh):
    wide = Mesh(mesh.devices.reshape(SIZES), ALL)
    lat, wid = ("x", "core"), ("z", "y")
    in_specs = (P(None, wid), P(wid), P(wid, lat), P(lat), P(lat, wid), P(None, lat), P())
    out_specs = (P(wid, lat), P(lat, wid), P(lat))
    return jax.shard_map(shards, mesh=wide, in_specs=in_specs, out_specs=out_specs, check_vma=False)
```

```python
import jax
import jax.numpy as jnp
from jax import lax
from jax.sharding import Mesh, PartitionSpec as P

F32 = jnp.float32
BF16 = jnp.bfloat16
ALL = ("x", "core", "z", "y")
SIZES = (4, 2, 4, 4)
SWAPS = ((1, 0, 3, 2), (3, 2, 1, 0))
UNITS = tuple((k, p) for k in range(2) for p in range(2))


def place(x, c, z, y):
    return ((x * 2 + c) * 4 + z) * 4 + y


def every():
    return [(x, c, z, y) for x in range(4) for c in range(2) for z in range(4) for y in range(4)]


def swap_perm(part, step):
    other = SWAPS[(part + step) % 2]
    pairs = []
    for x, c, z, y in every():
        along_y = (c == 0) == (step < 2)
        to = place(x, c, z, other[y]) if along_y else place(x, c, other[z], y)
        pairs.append((place(x, c, z, y), to))
    return pairs


def swap(value, part, step):
    return lax.ppermute(value, ALL, swap_perm(part, step))


def added(one, two):
    return (one.astype(F32) + two.astype(F32)).astype(BF16)


def tie(values):
    return lax.optimization_barrier(values)


def label_of(position, part):
    a, b = (position == 1) | (position == 2), position >= 2
    first, second = (a, b) if part == 0 else (b, a)
    return 2 * first.astype(jnp.int32) + second.astype(jnp.int32)


def outer_sum(low, high, part):
    value = added(low, swap(high, part, 0))
    half = value.shape[0] // 2
    return added(value[:half], swap(value[half:], part, 1))


def inner_sum(value, part):
    value = added(value, swap(value, part, 2))
    return value.astype(F32) + swap(value, part, 3).astype(F32)


def reduce_all(low, high):
    value = tie([outer_sum(low[u], high[u], p) for u, (k, p) in enumerate(UNITS)])
    return tie([inner_sum(value[u], p) for u, (k, p) in enumerate(UNITS)])


def gather_all(mine):
    first = [jnp.concatenate([mine[u], swap(mine[u], p, 1)], 0) for u, (k, p) in enumerate(UNITS)]
    second = [swap(first[u], p, 0) for u, (k, p) in enumerate(UNITS)]
    return first, second


def units_of(value):
    size = value.shape[0] // 4
    return [value[u * size : (u + 1) * size] for u in range(4)]


def shards(residual, dec_bias, enc_weight, enc_bias, dec_weight, act_mask, boundaries):
    rows = residual.shape[0]
    block = enc_weight.shape[1]
    x, c, z, y = (lax.axis_index(a) for a in ALL)
    lat_index = x * 2 + c
    scale = 2.0 / rows
    order = jnp.arange(boundaries.shape[0], dtype=jnp.int32)
    offset = jnp.sum(jnp.where(order == lat_index, boundaries, 0)) - lat_index * block
    column = jnp.arange(block, dtype=jnp.int32)
    inside = column < offset
    keep = inside.astype(BF16)
    above = (7 - lat_index).astype(F32)
    labels = [label_of(jnp.where(c == 0, y, z), p) for p in (0, 1)]
    turns = [jnp.bitwise_xor(label_of(jnp.where(c == 0, z, y), p), labels[p]) for p in (0, 1)]

    at = jnp.arange(rows, dtype=jnp.int32)
    half, unit, inner, row = at // 256, (at // 64) % 4, (at // 32) % 2, at % 32
    label = jnp.where(unit % 2 == 0, labels[0], labels[1])
    source = unit * 128 + jnp.bitwise_xor(half * 2 + inner, label) * 32 + row
    turn = jnp.bitwise_xor(half * 2 + inner, jnp.where(unit % 2 == 0, turns[0], turns[1]))
    theirs = (turn // 2) * 256 + unit * 64 + (turn % 2) * 32 + row
    turned = (theirs[:, None] == at[None, :]).astype(BF16)
    chosen = (source[:, None] == at[None, :]).astype(BF16)
    resid = jnp.dot(chosen, residual, preferred_element_type=F32)
    centred = (resid - dec_bias).astype(BF16)
    base = dec_bias - resid

    def encode(h):
        return units_of(jnp.dot(centred[h * 256 : h * 256 + 256], enc_weight, preferred_element_type=F32).astype(BF16))

    high = encode(1)
    low = encode(0)
    masks = [lax.dynamic_slice_in_dim(act_mask, u * 128 + labels[p] * 32, 32, 0).astype(BF16) for u, (k, p) in enumerate(UNITS)]
    value = reduce_all(low, high)
    masks = tie(masks)
    mine = [(m.astype(F32) * (v + enc_bias)).astype(BF16) for m, v in zip(masks, value)]
    pieces = gather_all(tie(mine))
    latents = [jnp.concatenate(v, 0) for v in pieces]

    def decode(latents):
        total = jnp.dot(latents, dec_weight, preferred_element_type=F32)
        lower = jnp.dot(latents * keep[None, :], dec_weight, preferred_element_type=F32)
        upper = above * total + lower
        total_b, upper_b = total.astype(BF16), upper.astype(BF16)
        before, rest = 0.0, 0.0
        for k in (2, 1, 3):
            out = jnp.where(x + k < 4, total_b, upper_b)
            got = lax.ppermute(out, "x", [(i, (i + k) % 4) for i in range(4)]).astype(F32)
            before = before + jnp.where(x >= k, got, 0.0)
            rest = rest + jnp.where(x < k, got, 0.0)
        give = (before + jnp.where(c == 0, total, 0.0)).astype(BF16), (rest + jnp.where(c == 1, upper, 0.0)).astype(BF16)
        got = lax.ppermute(jnp.concatenate(give, 0), "core", [(0, 1), (1, 0)])
        return total, upper, before, rest, got

    parts = [decode(v) for v in latents]
    got = [jnp.concatenate([parts[h][4][i * 256 : i * 256 + 256] for h in (0, 1)], 0) for i in (0, 1)]

    def level(h):
        total, upper, before, rest, _ = parts[h]
        mine = turned[h * 256 : h * 256 + 256]
        first = base[h * 256 : h * 256 + 256] + before + jnp.dot(mine, got[0], preferred_element_type=F32)
        rest = rest + jnp.dot(mine, got[1], preferred_element_type=F32)
        return ((above + 1.0) * first + upper + rest).astype(BF16), (above * (first + total) + rest).astype(BF16)

    def through(pair):
        dims = (((1,), (1,)), ((), ()))
        one, two = (lax.dot_general(v, dec_weight, dims, preferred_element_type=F32) for v in pair)
        return units_of(jnp.where(inside[None, :], one, two).astype(BF16))

    levels = {h: level(h) for h in (1, 0)}
    high = through(levels[1])
    low = through(levels[0])
    value = reduce_all(low, high)
    mine = [(m.astype(F32) * (scale * v)).astype(BF16) for m, v in zip(masks, value)]
    grads = gather_all(tie(mine))

    dims = (((0,), (0,)), ((), ()))
    latents = jnp.concatenate(latents, 0)
    one, two = (
        lax.dot_general(latents, jnp.concatenate([levels[0][i], levels[1][i]], 0), dims, preferred_element_type=F32)
        for i in (0, 1)
    )
    grad_dec = (scale * jnp.where(inside[:, None], one, two)).astype(BF16)
    grad_pre = jnp.concatenate(grads[0] + grads[1], 0)
    grad_enc = lax.dot_general(centred, grad_pre, dims, preferred_element_type=F32).astype(BF16)
    sums = [jnp.sum(jnp.concatenate(g, 0).astype(F32).reshape(4, 2, 32, block), axis=2) for g in grads]
    grad_benc = 0.0
    for u, (k, p) in enumerate(UNITS):
        blocks = [sums[j // 2][u, j % 2] for j in range(4)]
        for t in range(4):
            j = jnp.bitwise_xor(labels[p], t)
            pair = [jnp.where(j % 2 == 0, blocks[2 * i], blocks[2 * i + 1]) for i in (0, 1)]
            grad_benc = grad_benc + jnp.where(j < 2, pair[0], pair[1])
    return (grad_enc, grad_dec, grad_benc)


def solution(mesh):
    wide = Mesh(mesh.devices.reshape(SIZES), ALL)
    lat, wid = ("x", "core"), ("z", "y")
    in_specs = (P(None, wid), P(wid), P(wid, lat), P(lat), P(lat, wid), P(None, lat), P())
    out_specs = (P(wid, lat), P(lat, wid), P(lat))
    return jax.shard_map(shards, mesh=wide, in_specs=in_specs, out_specs=out_specs, check_vma=False)
```

```python
import jax
import jax.numpy as jnp
from jax import lax
from jax.sharding import Mesh, PartitionSpec as P

F32 = jnp.float32
BF16 = jnp.bfloat16
ALL = ("x", "core", "z", "y")
SIZES = (4, 2, 4, 4)
SWAPS = ((1, 0, 3, 2), (3, 2, 1, 0))
UNITS = tuple((k, p) for k in range(2) for p in range(2))


def place(x, c, z, y):
    return ((x * 2 + c) * 4 + z) * 4 + y


def every():
    return [(x, c, z, y) for x in range(4) for c in range(2) for z in range(4) for y in range(4)]


def swap_perm(part, step):
    other = SWAPS[(part + step) % 2]
    pairs = []
    for x, c, z, y in every():
        along_y = (c == 0) == (step < 2)
        to = place(x, c, z, other[y]) if along_y else place(x, c, other[z], y)
        pairs.append((place(x, c, z, y), to))
    return pairs


def swap(value, part, step):
    return lax.ppermute(value, ALL, swap_perm(part, step))


def added(one, two):
    return (one.astype(F32) + two.astype(F32)).astype(BF16)


def tie(values):
    return lax.optimization_barrier(values)


def label_of(position, part):
    a, b = (position == 1) | (position == 2), position >= 2
    first, second = (a, b) if part == 0 else (b, a)
    return 2 * first.astype(jnp.int32) + second.astype(jnp.int32)


def outer_sum(low, high, part):
    value = added(low, swap(high, part, 0))
    half = value.shape[0] // 2
    return added(value[:half], swap(value[half:], part, 1))


def inner_sum(value, part):
    value = added(value, swap(value, part, 2))
    return value.astype(F32) + swap(value, part, 3).astype(F32)


def reduce_all(low, high):
    value = tie([outer_sum(low[u], high[u], p) for u, (k, p) in enumerate(UNITS)])
    return tie([inner_sum(value[u], p) for u, (k, p) in enumerate(UNITS)])


def gather_all(mine):
    first = [jnp.concatenate([mine[u], swap(mine[u], p, 1)], 0) for u, (k, p) in enumerate(UNITS)]
    second = [swap(first[u], p, 0) for u, (k, p) in enumerate(UNITS)]
    return first, second


def units_of(value):
    size = value.shape[0] // 4
    return [value[u * size : (u + 1) * size] for u in range(4)]


def shards(residual, dec_bias, enc_weight, enc_bias, dec_weight, act_mask, boundaries):
    rows = residual.shape[0]
    block = enc_weight.shape[1]
    x, c, z, y = (lax.axis_index(a) for a in ALL)
    lat_index = x * 2 + c
    scale = 2.0 / rows
    order = jnp.arange(boundaries.shape[0], dtype=jnp.int32)
    offset = jnp.sum(jnp.where(order == lat_index, boundaries, 0)) - lat_index * block
    column = jnp.arange(block, dtype=jnp.int32)
    inside = column < offset
    keep = inside.astype(BF16)
    above = (7 - lat_index).astype(F32)
    labels = [label_of(jnp.where(c == 0, y, z), p) for p in (0, 1)]
    turns = [jnp.bitwise_xor(label_of(jnp.where(c == 0, z, y), p), labels[p]) for p in (0, 1)]

    at = jnp.arange(rows, dtype=jnp.int32)
    half, unit, inner, row = at // 256, (at // 64) % 4, (at // 32) % 2, at % 32
    label = jnp.where(unit % 2 == 0, labels[0], labels[1])
    source = unit * 128 + jnp.bitwise_xor(half * 2 + inner, label) * 32 + row
    turn = jnp.bitwise_xor(half * 2 + inner, jnp.where(unit % 2 == 0, turns[0], turns[1]))
    theirs = (turn // 2) * 256 + unit * 64 + (turn % 2) * 32 + row
    turned = (theirs[:, None] == at[None, :]).astype(BF16)
    chosen = (source[:, None] == at[None, :]).astype(BF16)
    resid = jnp.dot(chosen, residual, preferred_element_type=F32)
    centred = (resid - dec_bias).astype(BF16)
    base = dec_bias - resid

    def encode(h):
        return units_of(jnp.dot(centred[h * 256 : h * 256 + 256], enc_weight, preferred_element_type=F32).astype(BF16))

    partial_value = jnp.dot(centred, enc_weight, preferred_element_type=F32).astype(BF16)
    low, high = units_of(partial_value[:256]), units_of(partial_value[256:])
    masks = [lax.dynamic_slice_in_dim(act_mask, u * 128 + labels[p] * 32, 32, 0).astype(BF16) for u, (k, p) in enumerate(UNITS)]
    low, masks = tie((low, masks))
    value = reduce_all(low, high)
    mine = [(m.astype(F32) * (v + enc_bias)).astype(BF16) for m, v in zip(masks, value)]
    pieces = gather_all(tie(mine))
    latents = [jnp.concatenate(v, 0) for v in pieces]

    def decode(latents):
        total = jnp.dot(latents, dec_weight, preferred_element_type=F32)
        lower = jnp.dot(latents * keep[None, :], dec_weight, preferred_element_type=F32)
        upper = above * total + lower
        total_b, upper_b = total.astype(BF16), upper.astype(BF16)
        before, rest = 0.0, 0.0
        for k in (2, 1, 3):
            out = jnp.where(x + k < 4, total_b, upper_b)
            got = lax.ppermute(out, "x", [(i, (i + k) % 4) for i in range(4)]).astype(F32)
            before = before + jnp.where(x >= k, got, 0.0)
            rest = rest + jnp.where(x < k, got, 0.0)
        give = (before + jnp.where(c == 0, total, 0.0)).astype(BF16), (rest + jnp.where(c == 1, upper, 0.0)).astype(BF16)
        got = lax.ppermute(jnp.concatenate(give, 0), "core", [(0, 1), (1, 0)])
        return total, upper, before, rest, got

    parts = [decode(v) for v in latents]
    got = [jnp.concatenate([parts[h][4][i * 256 : i * 256 + 256] for h in (0, 1)], 0) for i in (0, 1)]

    def level(h):
        total, upper, before, rest, _ = parts[h]
        mine = turned[h * 256 : h * 256 + 256]
        first = base[h * 256 : h * 256 + 256] + before + jnp.dot(mine, got[0], preferred_element_type=F32)
        rest = rest + jnp.dot(mine, got[1], preferred_element_type=F32)
        return ((above + 1.0) * first + upper + rest).astype(BF16), (above * (first + total) + rest).astype(BF16)

    def through(pair):
        dims = (((1,), (1,)), ((), ()))
        one, two = (lax.dot_general(v, dec_weight, dims, preferred_element_type=F32) for v in pair)
        return units_of(jnp.where(inside[None, :], one, two).astype(BF16))

    levels = {h: level(h) for h in (1, 0)}
    high = through(levels[1])
    low = tie(through(levels[0]))
    value = reduce_all(low, high)
    mine = [(m.astype(F32) * (scale * v)).astype(BF16) for m, v in zip(masks, value)]
    grads = gather_all(tie(mine))

    dims = (((0,), (0,)), ((), ()))
    latents = tie((latents, grads[0]))[0]
    latents = jnp.concatenate(latents, 0)
    one, two = (
        lax.dot_general(latents, jnp.concatenate([levels[0][i], levels[1][i]], 0), dims, preferred_element_type=F32)
        for i in (0, 1)
    )
    grad_dec = (scale * jnp.where(inside[:, None], one, two)).astype(BF16)
    grad_pre = jnp.concatenate(grads[0] + grads[1], 0)
    grad_enc = lax.dot_general(centred, grad_pre, dims, preferred_element_type=F32).astype(BF16)
    sums = [jnp.sum(jnp.concatenate(g, 0).astype(F32).reshape(4, 2, 32, block), axis=2) for g in grads]
    grad_benc = 0.0
    for u, (k, p) in enumerate(UNITS):
        blocks = [sums[j // 2][u, j % 2] for j in range(4)]
        for t in range(4):
            j = jnp.bitwise_xor(labels[p], t)
            pair = [jnp.where(j % 2 == 0, blocks[2 * i], blocks[2 * i + 1]) for i in (0, 1)]
            grad_benc = grad_benc + jnp.where(j < 2, pair[0], pair[1])
    return (grad_enc, grad_dec, grad_benc)


def solution(mesh):
    wide = Mesh(mesh.devices.reshape(SIZES), ALL)
    lat, wid = ("x", "core"), ("z", "y")
    in_specs = (P(None, wid), P(wid), P(wid, lat), P(lat), P(lat, wid), P(None, lat), P())
    out_specs = (P(wid, lat), P(lat, wid), P(lat))
    return jax.shard_map(shards, mesh=wide, in_specs=in_specs, out_specs=out_specs, check_vma=False)
```

```python
import jax
import jax.numpy as jnp
from jax import lax
from jax.sharding import Mesh, PartitionSpec as P

F32 = jnp.float32
BF16 = jnp.bfloat16
ALL = ("x", "core", "z", "y")
SIZES = (4, 2, 4, 4)
SWAPS = ((1, 0, 3, 2), (3, 2, 1, 0))
UNITS = tuple((k, p) for k in range(2) for p in range(2))


def place(x, c, z, y):
    return ((x * 2 + c) * 4 + z) * 4 + y


def every():
    return [(x, c, z, y) for x in range(4) for c in range(2) for z in range(4) for y in range(4)]


def swap_perm(part, step):
    other = SWAPS[(part + step) % 2]
    pairs = []
    for x, c, z, y in every():
        along_y = (c == 0) == (step < 2)
        to = place(x, c, z, other[y]) if along_y else place(x, c, other[z], y)
        pairs.append((place(x, c, z, y), to))
    return pairs


def swap(value, part, step):
    return lax.ppermute(value, ALL, swap_perm(part, step))


def added(one, two):
    return (one.astype(F32) + two.astype(F32)).astype(BF16)


def tie(values):
    return lax.optimization_barrier(values)


def label_of(position, part):
    a, b = (position == 1) | (position == 2), position >= 2
    first, second = (a, b) if part == 0 else (b, a)
    return 2 * first.astype(jnp.int32) + second.astype(jnp.int32)


def outer_sum(low, high, part):
    value = added(low, swap(high, part, 0))
    half = value.shape[0] // 2
    return added(value[:half], swap(value[half:], part, 1))


def inner_sum(value, part):
    value = added(value, swap(value, part, 2))
    return value.astype(F32) + swap(value, part, 3).astype(F32)


def reduce_all(low, high):
    value = tie([outer_sum(low[u], high[u], p) for u, (k, p) in enumerate(UNITS)])
    return tie([inner_sum(value[u], p) for u, (k, p) in enumerate(UNITS)])


def gather_all(mine):
    first = [jnp.concatenate([mine[u], swap(mine[u], p, 1)], 0) for u, (k, p) in enumerate(UNITS)]
    second = [swap(first[u], p, 0) for u, (k, p) in enumerate(UNITS)]
    return first, second


def units_of(value):
    size = value.shape[0] // 4
    return [value[u * size : (u + 1) * size] for u in range(4)]


def shards(residual, dec_bias, enc_weight, enc_bias, dec_weight, act_mask, boundaries):
    rows = residual.shape[0]
    block = enc_weight.shape[1]
    x, c, z, y = (lax.axis_index(a) for a in ALL)
    lat_index = x * 2 + c
    scale = 2.0 / rows
    order = jnp.arange(boundaries.shape[0], dtype=jnp.int32)
    offset = jnp.sum(jnp.where(order == lat_index, boundaries, 0)) - lat_index * block
    column = jnp.arange(block, dtype=jnp.int32)
    inside = column < offset
    keep = inside.astype(BF16)
    above = (7 - lat_index).astype(F32)
    labels = [label_of(jnp.where(c == 0, y, z), p) for p in (0, 1)]
    turns = [jnp.bitwise_xor(label_of(jnp.where(c == 0, z, y), p), labels[p]) for p in (0, 1)]

    at = jnp.arange(rows, dtype=jnp.int32)
    half, unit, inner, row = at // 256, (at // 64) % 4, (at // 32) % 2, at % 32
    label = jnp.where(unit % 2 == 0, labels[0], labels[1])
    source = unit * 128 + jnp.bitwise_xor(half * 2 + inner, label) * 32 + row
    turn = jnp.bitwise_xor(half * 2 + inner, jnp.where(unit % 2 == 0, turns[0], turns[1]))
    theirs = (turn // 2) * 256 + unit * 64 + (turn % 2) * 32 + row
    turned = (theirs[:, None] == at[None, :]).astype(BF16)
    chosen = (source[:, None] == at[None, :]).astype(BF16)
    resid = jnp.dot(chosen, residual, preferred_element_type=F32)
    centred = (resid - dec_bias).astype(BF16)
    base = dec_bias - resid

    def encode(h):
        return units_of(jnp.dot(centred[h * 256 : h * 256 + 256], enc_weight, preferred_element_type=F32).astype(BF16))

    partial_value = jnp.dot(centred, enc_weight, preferred_element_type=F32).astype(BF16)
    high = units_of(partial_value[256:])
    masks = [lax.dynamic_slice_in_dim(act_mask, u * 128 + labels[p] * 32, 32, 0).astype(BF16) for u, (k, p) in enumerate(UNITS)]
    later, masks = tie((partial_value, masks))
    low = tie(units_of(later[:256]))
    value = reduce_all(low, high)
    mine = [(m.astype(F32) * (v + enc_bias)).astype(BF16) for m, v in zip(masks, value)]
    pieces = gather_all(tie(mine))
    latents = [jnp.concatenate(v, 0) for v in pieces]

    def decode(latents):
        total = jnp.dot(latents, dec_weight, preferred_element_type=F32)
        lower = jnp.dot(latents * keep[None, :], dec_weight, preferred_element_type=F32)
        upper = above * total + lower
        total_b, upper_b = total.astype(BF16), upper.astype(BF16)
        before, rest = 0.0, 0.0
        for k in (2, 1, 3):
            out = jnp.where(x + k < 4, total_b, upper_b)
            got = lax.ppermute(out, "x", [(i, (i + k) % 4) for i in range(4)]).astype(F32)
            before = before + jnp.where(x >= k, got, 0.0)
            rest = rest + jnp.where(x < k, got, 0.0)
        give = (before + jnp.where(c == 0, total, 0.0)).astype(BF16), (rest + jnp.where(c == 1, upper, 0.0)).astype(BF16)
        got = lax.ppermute(jnp.concatenate(give, 0), "core", [(0, 1), (1, 0)])
        return total, upper, before, rest, got

    parts = [decode(v) for v in latents]
    got = [jnp.concatenate([parts[h][4][i * 256 : i * 256 + 256] for h in (0, 1)], 0) for i in (0, 1)]

    def level(h):
        total, upper, before, rest, _ = parts[h]
        mine = turned[h * 256 : h * 256 + 256]
        first = base[h * 256 : h * 256 + 256] + before + jnp.dot(mine, got[0], preferred_element_type=F32)
        rest = rest + jnp.dot(mine, got[1], preferred_element_type=F32)
        return ((above + 1.0) * first + upper + rest).astype(BF16), (above * (first + total) + rest).astype(BF16)

    def through(pair):
        dims = (((1,), (1,)), ((), ()))
        one, two = (lax.dot_general(v, dec_weight, dims, preferred_element_type=F32) for v in pair)
        return units_of(jnp.where(inside[None, :], one, two).astype(BF16))

    levels = {h: level(h) for h in (1, 0)}
    high = through(levels[1])
    low = tie(through(levels[0]))
    value = reduce_all(low, high)
    mine = [(m.astype(F32) * (scale * v)).astype(BF16) for m, v in zip(masks, value)]
    grads = gather_all(tie(mine))

    dims = (((0,), (0,)), ((), ()))
    latents = tie((latents, grads[0]))[0]
    latents = jnp.concatenate(latents, 0)
    one, two = (
        lax.dot_general(latents, jnp.concatenate([levels[0][i], levels[1][i]], 0), dims, preferred_element_type=F32)
        for i in (0, 1)
    )
    grad_dec = (scale * jnp.where(inside[:, None], one, two)).astype(BF16)
    grad_pre = jnp.concatenate(grads[0] + grads[1], 0)
    grad_enc = lax.dot_general(centred, grad_pre, dims, preferred_element_type=F32).astype(BF16)
    sums = [jnp.sum(jnp.concatenate(g, 0).astype(F32).reshape(4, 2, 32, block), axis=2) for g in grads]
    grad_benc = 0.0
    for u, (k, p) in enumerate(UNITS):
        blocks = [sums[j // 2][u, j % 2] for j in range(4)]
        for t in range(4):
            j = jnp.bitwise_xor(labels[p], t)
            pair = [jnp.where(j % 2 == 0, blocks[2 * i], blocks[2 * i + 1]) for i in (0, 1)]
            grad_benc = grad_benc + jnp.where(j < 2, pair[0], pair[1])
    return (grad_enc, grad_dec, grad_benc)


def solution(mesh):
    wide = Mesh(mesh.devices.reshape(SIZES), ALL)
    lat, wid = ("x", "core"), ("z", "y")
    in_specs = (P(None, wid), P(wid), P(wid, lat), P(lat), P(lat, wid), P(None, lat), P())
    out_specs = (P(wid, lat), P(lat, wid), P(lat))
    return jax.shard_map(shards, mesh=wide, in_specs=in_specs, out_specs=out_specs, check_vma=False)
```
